32 devices in a mesh: gx: 8 (over z, core), gy: 4 (over y, x).
Axes of the slice: x: 2, y: 2, z: 4, core: 2. Of those that a mesh axis runs over, the one named last changes fastest.
Arguments:
- net_inputs: bfloat16 [25, 1572864], P(None, ('gx', 'gy')), may hold values from -6 to 6
- velocity: float32 [3, 1572864], P(None, ('gx', 'gy'))
- particle_mass: float32 [1572864], P(('gx', 'gy')), may hold values from 0.5 to 2
- block_column: int32 [12288], P(('gx', 'gy')), may hold values from 0 to 8191, as said below
- cell_height: int32 [1572864], P(('gx', 'gy')), may hold values from 0 to 127
- block_counts: int32 [32], replicated, may hold values from 48 to 384, as said below
- cotangent: float32 [3, 1572864], P(None, ('gx', 'gy'))
- input_weight: bfloat16 [80, 25], replicated, may hold values from -1.25 to 1.25
- input_bias: float32 [80], replicated, may hold values from -3 to 3
- middle_weight: bfloat16 [80, 80], replicated, may hold values from -0.625 to 0.625
- middle_bias: float32 [80], replicated, may hold values from -3 to 3
- output_weight: bfloat16 [9, 80], replicated, may hold values from -0.625 to 0.625
- output_bias: float32 [9], replicated, may hold values from -3 to 3
Outputs:
- new_velocity: float32 [3, 1572864], P(None, ('gx', 'gy'))
- input_weight_grad: float32 [80, 25], replicated
- input_bias_grad: float32 [80], replicated
- middle_weight_grad: float32 [80, 80], replicated
- middle_bias_grad: float32 [80], replicated
- output_weight_grad: float32 [9, 80], replicated
- output_bias_grad: float32 [9], replicated
The draws below stay inside these ranges and needn't reach their ends.
Inputs may be any that keep to these rules, and one draw needn't show every extreme that they name: `block_column`: the column of a block is 64 X + Y. Every block stored on the device at mesh position (i, j), i along gx, has X within i * 16 - 1 to i * 16 + 16 and Y within j * 16 - 1 to j * 16 + 16, both taken periodically over 128 and 64. `block_counts`: entry i * 4 + j counts the live blocks of the device at mesh position (i, j); they fill that device's first slots. One device, drawn from the seed, has all 384 live.
All inputs are finite; a program needn't handle non-finite values.
Results may differ from the reference program's by a relative error of at most 0.0056.
Values sent between devices are 32-bit elements; how exact they have to be, the bound alone decides.
A program may use at most 64 MiB of HBM per device.

```python
import math
import jax
import jax.numpy as jnp
from jax import lax

CX = 16
CY = 16
NZ = 128
PB = 384
BLOCK = 128
HID = 80
IN = 25
NX = 128
NY = 64
PARTS_SIZE = 1572864


def rising_field(key):
    tile_parts = PB * BLOCK
    tiles = PARTS_SIZE // tile_parts
    position = (jnp.arange(PARTS_SIZE) // tile_parts).astype(jnp.float32) / max(tiles - 1, 1)
    ramp_scale = 1.0 + 2.0 * position
    base_draw = jax.random.normal(key, (3, PARTS_SIZE), jnp.float32)
    return base_draw * ramp_scale


def draw_velocity(key, part):
    key = jax.random.fold_in(key, 11)
    return rising_field(key)


def draw_cotangent(key, part):
    key = jax.random.fold_in(key, 12)
    return rising_field(key)


def draw_block_column(key, part):
    key = jax.random.fold_in(key, 13)
    blocks = PARTS_SIZE // BLOCK
    tiles_y = NY // CY
    device = jnp.arange(blocks, dtype=jnp.int32) // PB
    tile_x = device // tiles_y
    tile_y = device % tiles_y
    key_x, key_y = jax.random.split(key)
    offset_x = jax.random.randint(key_x, (blocks,), -1, CX + 1, dtype=jnp.int32)
    offset_y = jax.random.randint(key_y, (blocks,), -1, CY + 1, dtype=jnp.int32)
    offset_x = offset_x.at[0].set(-1).at[1].set(0)
    offset_y = offset_y.at[0].set(-1).at[1].set(0)
    global_x = (tile_x * CX + offset_x) % NX
    global_y = (tile_y * CY + offset_y) % NY
    return (global_x * NY + global_y).astype(jnp.int32)


def draw_block_counts(key, part):
    key = jax.random.fold_in(key, 17)
    tiles = PARTS_SIZE // (PB * BLOCK)
    lowest = max(PB // 8, 1)
    key_count, key_full, key_low = jax.random.split(key, 3)
    counts_drawn = jax.random.randint(key_count, (tiles,), lowest, PB // 2 + 1, dtype=jnp.int32)
    full_device = jax.random.randint(key_full, (), 0, tiles, dtype=jnp.int32)
    low_device = (full_device + 1 + jax.random.randint(key_low, (), 0, max(tiles - 1, 1), dtype=jnp.int32)) % tiles
    positions = jnp.arange(tiles, dtype=jnp.int32)
    counts_drawn = jnp.where(positions == low_device, lowest, counts_drawn)
    counts_drawn = jnp.where(positions == full_device, PB, counts_drawn)
    return counts_drawn.astype(jnp.int32)


def plant(entries, rng, low, largest):
    extent = entries.shape
    spot = [jax.random.randint(jax.random.fold_in(rng, axis), (), 0, extent[axis]) for axis in range(len(extent))]
    entries = entries.at[tuple(spot)].set(low)
    longest = extent.index(max(extent))
    spot[longest] = (spot[longest] + 1) % extent[longest]
    return entries.at[tuple(spot)].set(largest)


def block_levels(key, shape, cuts, low, top_value):
    def one(dim, blocks):
        draws = jax.random.uniform(jax.random.fold_in(jax.random.fold_in(key, 6), dim), (blocks,), jnp.float32, low / len(cuts), top_value / len(cuts))
        return jnp.repeat(jnp.exp(draws), shape[dim] // blocks).reshape((-1,) + (1,) * (len(shape) - dim - 1))

    level = one(*cuts[0])
    for cut in cuts[1:]:
        level = level * one(*cut)
    return level


def scatter_about(key, shape, width, bound, cuts=(), kind=jnp.bfloat16):
    array = jax.random.normal(key, shape, jnp.float32) * width
    if len(cuts) > 0:
        array = block_levels(key, shape, cuts, -0.22, 0.18) * array
    return jnp.clip(array, min=-bound, max=bound).astype(kind)


def setup_inputs(seed: int = 0) -> dict:
    splits = jax.random.split(jax.random.key(seed), 14)
    net_inputs = scatter_about(splits[0], (IN, PARTS_SIZE), 1.0, 6.0, ((1, 32),))
    velocity = draw_velocity(jax.random.fold_in(splits[13], 71), 0)
    particle_mass = jnp.clip(jnp.exp(math.log(2.0) - 1.3862944 * jax.random.uniform(splits[2], (PARTS_SIZE,), jnp.float32) ** block_levels(splits[2], (PARTS_SIZE,), ((0, 32),), -0.2, 0.2)), 0.5, 2.0)
    block_column = draw_block_column(jax.random.fold_in(splits[13], 71), 0)
    cell_height = plant(jax.random.randint(splits[4], (PARTS_SIZE,), 0, NZ), jax.random.fold_in(splits[4], 1), 0, NZ - 1).astype(jnp.int32)
    block_counts = draw_block_counts(jax.random.fold_in(splits[13], 71), 0)
    cotangent = draw_cotangent(jax.random.fold_in(splits[13], 71), 0)
    input_weight = scatter_about(splits[7], (HID, IN), IN ** -0.5, 1.25)
    input_bias = scatter_about(splits[8], (HID,), 0.5, 3.0, (), jnp.float32)
    middle_weight = scatter_about(splits[9], (HID, HID), HID ** -0.5, 0.625)
    middle_bias = scatter_about(splits[10], (HID,), 0.5, 3.0, (), jnp.float32)
    output_weight = scatter_about(splits[11], (9, HID), HID ** -0.5, 0.625)
    output_bias = scatter_about(splits[12], (9,), 0.5, 3.0, (), jnp.float32)
    return {"net_inputs": net_inputs, "velocity": velocity, "particle_mass": particle_mass, "block_column": block_column, "cell_height": cell_height, "block_counts": block_counts, "cotangent": cotangent, "input_weight": input_weight, "input_bias": input_bias, "middle_weight": middle_weight, "middle_bias": middle_bias, "output_weight": output_weight, "output_bias": output_bias}


time_scale = 0.5
epsilon = 1e-06

def network(inputs, input_weight, input_bias, middle_weight, middle_bias, output_weight, output_bias):
    first = jnp.dot(input_weight, inputs, preferred_element_type=jnp.float32) + input_bias[:, None]
    first_act = jax.nn.silu(first).astype(jnp.bfloat16)
    second = jnp.dot(middle_weight, first_act, preferred_element_type=jnp.float32) + middle_bias[:, None]
    second_act = jax.nn.silu(second).astype(jnp.bfloat16)
    stress = jnp.dot(output_weight, second_act, preferred_element_type=jnp.float32) + output_bias[:, None]
    return (first, first_act, second, second_act, stress)

def silu_slope(values):
    sigmoid = jax.nn.sigmoid(values)
    return sigmoid * (1.0 + values * (1.0 - sigmoid))

def network_grads(inputs, stress_cot, input_weight, input_bias, middle_weight, middle_bias, output_weight, output_bias):
    first, first_act, second, second_act, stress = network(inputs, input_weight, input_bias, middle_weight, middle_bias, output_weight, output_bias)
    stress_cot_low = stress_cot.astype(jnp.bfloat16)
    output_weight_grad = jnp.dot(stress_cot_low, second_act.T, preferred_element_type=jnp.float32)
    output_bias_grad = lax.optimization_barrier(jnp.sum(stress_cot, axis=1))
    second_cot = jnp.dot(output_weight.T, stress_cot_low, preferred_element_type=jnp.float32) * silu_slope(second)
    second_low = second_cot.astype(jnp.bfloat16)
    middle_weight_grad = jnp.dot(second_low, first_act.T, preferred_element_type=jnp.float32)
    middle_bias_grad = lax.optimization_barrier(jnp.sum(second_cot, axis=1))
    first_cot = jnp.dot(middle_weight.T, second_low, preferred_element_type=jnp.float32) * silu_slope(first)
    first_low = first_cot.astype(jnp.bfloat16)
    input_weight_grad = jnp.dot(first_low, inputs.T, preferred_element_type=jnp.float32)
    input_bias_grad = lax.optimization_barrier(jnp.sum(first_cot, axis=1))
    return (input_weight_grad, input_bias_grad, middle_weight_grad, middle_bias_grad, output_weight_grad, output_bias_grad)

def central(field, axis):
    return 0.5 * (jnp.roll(field, -1, axis) - jnp.roll(field, 1, axis))

def vertical(field):
    widths = [(0, 0)] * (field.ndim - 1) + [(1, 1)]
    padded = jnp.pad(field, widths)
    return 0.5 * (padded[..., 2:] - padded[..., :-2])

def divergence(stress_grid):
    shaped = stress_grid.reshape((3, 3) + stress_grid.shape[1:])
    return central(shaped[:, 0], 1) + central(shaped[:, 1], 2) + vertical(shaped[:, 2])

def stress_adjoint(force_cot):
    stacked = jnp.stack([-central(force_cot, 1), -central(force_cot, 2), -vertical(force_cot)], axis=1)
    return stacked.reshape((9,) + force_cot.shape[1:])

def reference(net_inputs, velocity, particle_mass, block_column, cell_height, block_counts, cotangent, input_weight, input_bias, middle_weight, middle_bias, output_weight, output_bias):
    params = (input_weight, input_bias, middle_weight, middle_bias, output_weight, output_bias)
    tile_parts = PB * BLOCK
    tiles = PARTS_SIZE // tile_parts
    block_index = jnp.arange(PARTS_SIZE // BLOCK, dtype=jnp.int32)
    slot_index = block_index % PB
    owner = block_index // PB
    live_mask = jnp.repeat((slot_index < block_counts[owner]).astype(jnp.float32), BLOCK)
    weight = particle_mass * live_mask
    column = jnp.repeat(block_column, BLOCK)
    flat_index = (column * NZ + cell_height).astype(jnp.int32)
    by_tile = net_inputs.reshape(IN, tiles, tile_parts).transpose(1, 0, 2)
    stress = lax.map(lambda tile_input: network(tile_input, *params)[4], by_tile)
    stress = stress.transpose(1, 0, 2).reshape(9, PARTS_SIZE)
    values = jnp.concatenate([weight * velocity, weight[None], weight * stress], axis=0)
    totals = jnp.zeros((13, NX * NY * NZ), jnp.float32).at[:, flat_index].add(values)
    totals = totals.reshape(13, NX, NY, NZ)
    inverse = 1.0 / (totals[3] + 1.0)
    drift = totals[0:3] * inverse
    energy = jnp.sum(drift * drift) / (NX * NY * NZ)
    step_size = time_scale / jnp.sqrt(energy + epsilon)
    force = divergence(totals[4:13])
    grid_velocity = drift + step_size * inverse * force
    new_velocity = grid_velocity.reshape(3, -1)[:, flat_index]
    velocity_cot = jnp.zeros((3, NX * NY * NZ), jnp.float32).at[:, flat_index].add(cotangent)
    velocity_cot = velocity_cot.reshape(3, NX, NY, NZ)
    force_cot = step_size * inverse * velocity_cot
    stress_cot_grid = stress_adjoint(force_cot)
    stress_cot = stress_cot_grid.reshape(9, -1)[:, flat_index] * weight
    cot_tiles = stress_cot.reshape(9, tiles, tile_parts).transpose(1, 0, 2)

    def accumulate(running, pieces):
        fresh_grads = network_grads(pieces[0], pieces[1], *params)
        return (tuple((earlier_term + later_term for earlier_term, later_term in zip(running, fresh_grads))), None)
    initial = (jnp.zeros((HID, IN), jnp.float32), jnp.zeros((HID,), jnp.float32), jnp.zeros((HID, HID), jnp.float32), jnp.zeros((HID,), jnp.float32), jnp.zeros((9, HID), jnp.float32), jnp.zeros((9,), jnp.float32))
    summed, unused = lax.scan(accumulate, initial, (by_tile, cot_tiles))
    live_total = jnp.sum(block_counts).astype(jnp.float32) * BLOCK
    root_total = jnp.sqrt(live_total)
    return (new_velocity, summed[0] / root_total, summed[1] / root_total, summed[2] / root_total, summed[3] / root_total, summed[4] / root_total, summed[5] / root_total)
```

```python
import jax
import jax.numpy as jnp
from jax import lax
from jax.experimental import pallas as pl
from jax.experimental.pallas import tpu as pltpu
from jax.sharding import PartitionSpec as P

CX = 16
CY = 16
NZ = 128
PB = 384
BLOCK = 128
GROUP = 16
ROWS = 16
SPAN = GROUP * BLOCK


time_scale = 0.5
epsilon = 1e-06


def sigmoid(values):
    return 0.5 * jnp.tanh(0.5 * values) + 0.5


def dot(left, right):
    return jnp.dot(left, right, preferred_element_type=jnp.float32)


def dot_nt(left, right):
    return lax.dot_general(
        left, right, (((1,), (1,)), ((), ())), preferred_element_type=jnp.float32
    )


def split_halves(values):
    high = values.astype(jnp.bfloat16)
    low = (values - high.astype(jnp.float32)).astype(jnp.bfloat16)
    return jnp.concatenate([high, low], axis=0)


def height_selector(heights):
    level = lax.broadcasted_iota(jnp.int32, (NZ, BLOCK), 0)
    return jnp.where(level == heights, 1.0, 0.0).astype(jnp.bfloat16)


def deposit_kernel(
    column_ref,
    live_ref,
    inputs_ref,
    velocity_ref,
    mass_ref,
    height_ref,
    cot_ref,
    w1_ref,
    b1_ref,
    w2_ref,
    b2_ref,
    w3_ref,
    b3_ref,
    sums_ref,
):
    turn = pl.program_id(0)

    @pl.when(turn == 0)
    def _():
        sums_ref[...] = jnp.zeros_like(sums_ref)

    first = dot(w1_ref[...], inputs_ref[...]) + b1_ref[...]
    first_act = (first * sigmoid(first)).astype(jnp.bfloat16)
    second = dot(w2_ref[...], first_act) + b2_ref[...]
    second_act = (second * sigmoid(second)).astype(jnp.bfloat16)
    stress = dot(w3_ref[...], second_act) + b3_ref[...]
    gap = jnp.zeros((ROWS - 6, SPAN), jnp.float32)
    values = stress + jnp.concatenate([velocity_ref[...], gap, cot_ref[...]], axis=0)
    weighted = lax.broadcasted_iota(jnp.int32, (ROWS, BLOCK), 0) < 13
    for block in range(GROUP):
        index = turn * GROUP + block
        live = jnp.where(index < live_ref[0], 1.0, 0.0)
        weight = mass_ref[block : block + 1, :] * live
        piece = values[:, block * BLOCK : (block + 1) * BLOCK] * jnp.where(weighted, weight, 1.0)
        selector = height_selector(height_ref[block : block + 1, :])
        both = dot_nt(split_halves(piece), selector)
        column = column_ref[index]
        sums_ref[column] = sums_ref[column] + (both[:ROWS] + both[ROWS:])


def fill_grid(step, wide_ref, scaled_ref, grid_ref):
    wide_x, wide_y = CX + 4, CY + 4
    cots = lax.broadcasted_iota(jnp.int32, (wide_y, ROWS, NZ), 1) >= 13
    lane = lax.broadcasted_iota(jnp.int32, (CY + 2, ROWS, NZ), 2)

    def scale_row(x, carry):
        totals = wide_ref[x]
        inverse = 1.0 / (totals[:, 3:4] + 1.0)
        scaled_ref[x] = totals * jnp.where(cots, inverse, 1.0)
        return carry

    lax.fori_loop(0, wide_x, scale_row, 0)

    def fill_row(x, carry):
        here = scaled_ref[x + 1]
        middle = here[1:-1]
        diff_x = 0.5 * (scaled_ref[x + 2, 1 : wide_y - 1] - scaled_ref[x, 1 : wide_y - 1])
        diff_y = 0.5 * (here[2:] - here[:-2])
        above = jnp.where(lane < NZ - 1, pltpu.roll(middle, NZ - 1, 2), 0.0)
        below = jnp.where(lane > 0, pltpu.roll(middle, 1, 2), 0.0)
        diff_z = 0.5 * (above - below)
        inverse = 1.0 / (middle[:, 3:4] + 1.0)
        force = diff_x[:, 4:7] + diff_y[:, 7:10] + diff_z[:, 10:13]
        speed = inverse * middle[:, 0:3] + step * (inverse * force)
        cot_rows = [-step * diff[:, 13:16] for diff in (diff_x, diff_y, diff_z)]
        rows = jnp.concatenate(
            [speed, jnp.zeros_like(inverse)] + cot_rows + [jnp.zeros_like(speed)], axis=1
        )
        grid_ref[pl.ds(x * (CY + 2), CY + 2)] = rows
        return carry

    lax.fori_loop(0, CX + 2, fill_row, 0)


def gather_kernel(
    column_ref,
    live_ref,
    step_ref,
    inputs_ref,
    mass_ref,
    height_ref,
    wide_ref,
    w1_ref,
    b1_ref,
    w2_ref,
    b2_ref,
    w3t_ref,
    w2t_ref,
    velocity_ref,
    gin_ref,
    gmid_ref,
    gout_ref,
    bin_ref,
    bmid_ref,
    bout_ref,
    scaled_ref,
    grid_ref,
):
    turn = pl.program_id(0)
    step = step_ref[0]

    @pl.when(turn == 0)
    def _():
        for ref in (gin_ref, gmid_ref, gout_ref, bin_ref, bmid_ref, bout_ref):
            ref[...] = jnp.zeros_like(ref)
        fill_grid(step, wide_ref, scaled_ref, grid_ref)

    picked_cols, cot_cols = [], []
    for block in range(GROUP):
        index = turn * GROUP + block
        live = jnp.where(index < live_ref[0], 1.0, 0.0)
        weight = mass_ref[block : block + 1, :] * live
        selector = height_selector(height_ref[block : block + 1, :])
        both = dot(split_halves(grid_ref[column_ref[index]]), selector)
        picked = both[:ROWS] + both[ROWS:]
        picked_cols.append(picked)
        cot_cols.append(picked * weight)
    picked = jnp.concatenate(picked_cols, axis=1)
    stress_cot = jnp.concatenate(cot_cols, axis=1)
    velocity_ref[...] = picked[0:3]

    inputs = inputs_ref[...]
    first = dot(w1_ref[...], inputs) + b1_ref[...]
    first_sig = sigmoid(first)
    first_act = (first * first_sig).astype(jnp.bfloat16)
    second = dot(w2_ref[...], first_act) + b2_ref[...]
    second_sig = sigmoid(second)
    second_act = (second * second_sig).astype(jnp.bfloat16)
    cot_low = stress_cot.astype(jnp.bfloat16)
    second_cot = dot(w3t_ref[...], cot_low) * (second_sig * (1.0 + second * (1.0 - second_sig)))
    second_low = second_cot.astype(jnp.bfloat16)
    first_cot = dot(w2t_ref[...], second_low) * (first_sig * (1.0 + first * (1.0 - first_sig)))
    first_low = first_cot.astype(jnp.bfloat16)
    gin_ref[...] += dot_nt(first_low, inputs)
    gmid_ref[...] += dot_nt(second_low, first_act)
    gout_ref[...] += dot_nt(second_act, cot_low)

    def lanes(values):
        return sum(values[:, k * BLOCK : (k + 1) * BLOCK] for k in range(GROUP))

    bin_ref[...] += lanes(first_cot)
    bmid_ref[...] += lanes(second_cot)
    bout_ref[...] += lanes(stress_cot)


def greet_lines(me_x, me_y, size_x, size_y):
    barrier = pltpu.get_barrier_semaphore()
    for d in range(1, size_y):
        pl.semaphore_signal(
            barrier,
            inc=1,
            device_id=(me_x, lax.rem(me_y + d, size_y)),
            device_id_type=pl.DeviceIdType.MESH,
        )
    for d in range(1, size_x):
        pl.semaphore_signal(
            barrier,
            inc=1,
            device_id=(lax.rem(me_x + d, size_x), me_y),
            device_id_type=pl.DeviceIdType.MESH,
        )
    pl.semaphore_wait(barrier, size_x + size_y - 2)


def remote(source, target, send, recv, device):
    return pltpu.make_async_remote_copy(
        src_ref=source,
        dst_ref=target,
        send_sem=send,
        recv_sem=recv,
        device_id=device,
        device_id_type=pl.DeviceIdType.MESH,
    )


def line_sum(slots, send, recv, me, size, target):
    copies = []
    for d in range(1, size):
        copy = remote(
            slots.at[me], slots.at[me], send.at[d], recv.at[me], target(lax.rem(me + d, size))
        )
        copy.start()
        copies.append(copy)
    for d in range(1, size):
        other = lax.rem(me + d, size)
        remote(
            slots.at[other], slots.at[other], send.at[d], recv.at[other], target(other)
        ).wait_recv()
    for copy in copies:
        copy.wait_send()
    total = slots[0]
    for k in range(1, size):
        total = total + slots[k]
    return total


def mesh_sum(values, y_slots, x_slots, y_send, y_recv, x_send, x_recv):
    me_x, me_y = lax.axis_index("gx"), lax.axis_index("gy")
    y_slots[me_y] = values
    x_slots[me_x] = line_sum(
        y_slots, y_send, y_recv, me_y, y_slots.shape[0], lambda other: (me_x, other)
    )
    return line_sum(x_slots, x_send, x_recv, me_x, x_slots.shape[0], lambda other: (other, me_y))


def sum_scratch(shape):
    size_x, size_y = lax.axis_size("gx"), lax.axis_size("gy")
    return [
        pltpu.VMEM((size_y,) + shape, jnp.float32),
        pltpu.VMEM((size_x,) + shape, jnp.float32),
        pltpu.SemaphoreType.DMA((size_y,)),
        pltpu.SemaphoreType.DMA((size_y,)),
        pltpu.SemaphoreType.DMA((size_x,)),
        pltpu.SemaphoreType.DMA((size_x,)),
    ]


def grads_kernel(gin_ref, gmid_ref, gout_ref, bin_ref, bmid_ref, bout_ref, out_ref, *slots):
    size_x, size_y = slots[1].shape[0], slots[0].shape[0]
    greet_lines(lax.axis_index("gx"), lax.axis_index("gy"), size_x, size_y)
    hidden = gin_ref.shape[0]
    bout = jnp.sum(bout_ref[...], axis=1, keepdims=True)
    parts = [
        gin_ref[...],
        jnp.sum(bin_ref[...], axis=1, keepdims=True),
        gmid_ref[...],
        jnp.sum(bmid_ref[...], axis=1, keepdims=True),
        gout_ref[...],
        jnp.concatenate([bout, jnp.zeros((hidden - ROWS, 1), jnp.float32)], axis=0),
    ]
    gap = out_ref.shape[1] - sum(part.shape[1] for part in parts)
    joined = jnp.concatenate(parts + [jnp.zeros((hidden, gap), jnp.float32)], axis=1)
    out_ref[...] = mesh_sum(joined, *slots)


def halo_kernel(
    sums_ref, wide_ref, energy_ref, x_halo, y_halo, halo_send, halo_recv, *slots
):
    size_x, size_y = slots[1].shape[0], slots[0].shape[0]
    me_x, me_y = lax.axis_index("gx"), lax.axis_index("gy")
    greet_lines(me_x, me_y, size_x, size_y)
    next_x, last_x = lax.rem(me_x + 1, size_x), lax.rem(me_x + size_x - 1, size_x)
    next_y, last_y = lax.rem(me_y + 1, size_y), lax.rem(me_y + size_y - 1, size_y)
    ends = CX + 2
    copies = [
        remote(
            sums_ref.at[pl.ds(ends - 3, 3)],
            x_halo.at[0],
            halo_send.at[0],
            halo_recv.at[0],
            (next_x, me_y),
        ),
        remote(
            sums_ref.at[pl.ds(0, 3)], x_halo.at[1], halo_send.at[1], halo_recv.at[1], (last_x, me_y)
        ),
    ]
    for copy in copies:
        copy.start()
    inner_y = pl.ds(1, CY + 2)

    def move(x, carry):
        wide_ref[x + 1, inner_y] = sums_ref[x]
        return carry

    lax.fori_loop(2, ends - 2, move, 0)
    for copy in copies:
        copy.wait()
    wide_ref[0, inner_y] = x_halo[0, 0]
    wide_ref[1, inner_y] = sums_ref[0] + x_halo[0, 1]
    wide_ref[2, inner_y] = sums_ref[1] + x_halo[0, 2]
    wide_ref[ends - 1, inner_y] = sums_ref[ends - 2] + x_halo[1, 0]
    wide_ref[ends, inner_y] = sums_ref[ends - 1] + x_halo[1, 1]
    wide_ref[ends + 1, inner_y] = x_halo[1, 2]
    edge = CY + 2
    copies = [
        remote(
            wide_ref.at[:, pl.ds(edge - 2, 3)],
            y_halo.at[0],
            halo_send.at[2],
            halo_recv.at[2],
            (me_x, next_y),
        ),
        remote(
            wide_ref.at[:, pl.ds(1, 3)], y_halo.at[1], halo_send.at[3], halo_recv.at[3], (me_x, last_y)
        ),
    ]
    for copy in copies:
        copy.start()
    for copy in copies:
        copy.wait()

    def fold(x, carry):
        wide_ref[x, 0] = y_halo[0, x, 0]
        wide_ref[x, 1] = wide_ref[x, 1] + y_halo[0, x, 1]
        wide_ref[x, 2] = wide_ref[x, 2] + y_halo[0, x, 2]
        wide_ref[x, edge - 1] = wide_ref[x, edge - 1] + y_halo[1, x, 0]
        wide_ref[x, edge] = wide_ref[x, edge] + y_halo[1, x, 1]
        wide_ref[x, edge + 1] = y_halo[1, x, 2]
        return carry

    lax.fori_loop(0, CX + 4, fold, 0)
    speeds = lax.broadcasted_iota(jnp.int32, (8, NZ), 0) < 3

    def energy_row(x, total):
        cells = wide_ref[x, 2 : CY + 2, 0:8]
        drift = cells * (1.0 / (cells[:, 3:4] + 1.0))
        return total + jnp.sum(drift * drift, axis=0)

    energy = lax.fori_loop(2, CX + 2, energy_row, jnp.zeros((8, NZ), jnp.float32))
    energy_ref[...] = mesh_sum(jnp.where(speeds, energy, 0.0), *slots)


def shards(
    net_inputs,
    velocity,
    particle_mass,
    block_column,
    cell_height,
    block_counts,
    cotangent,
    input_weight,
    input_bias,
    middle_weight,
    middle_bias,
    output_weight,
    output_bias,
):
    tiles_x, tiles_y = lax.axis_size("gx"), lax.axis_size("gy")
    index_x, index_y = lax.axis_index("gx"), lax.axis_index("gy")
    width_x, width_y = CX * tiles_x, CY * tiles_y
    hidden, rows_in = input_weight.shape
    live = lax.dynamic_slice_in_dim(block_counts, index_x * tiles_y + index_y, 1, 0)
    local_x = (block_column // width_y - index_x * CX + 1) % width_x
    local_y = (block_column % width_y - index_y * CY + 1) % width_y
    block_ext = local_x * (CY + 2) + local_y
    mass = particle_mass.reshape(PB, BLOCK)
    height = cell_height.reshape(PB, BLOCK)
    b1 = input_bias[:, None]
    b2 = middle_bias[:, None]
    turned = output_weight.reshape(3, 3, hidden).transpose(1, 0, 2).reshape(9, hidden)
    w3 = jnp.pad(turned, ((4, 3), (0, 0)))
    b3 = jnp.concatenate(
        [jnp.zeros((3,)), jnp.ones((1,)), output_bias.reshape(3, 3).T.reshape(9), jnp.zeros((3,))]
    ).astype(jnp.float32)[:, None]

    def whole(shape):
        return pl.BlockSpec(shape, lambda i, *_: (0,) * len(shape))

    def spread(rows):
        return pl.BlockSpec((rows, SPAN), lambda i, *_: (0, i))

    per_block = pl.BlockSpec((GROUP, BLOCK), lambda i, *_: (i, 0))
    params = pltpu.CompilerParams(vmem_limit_bytes=40 * 1024 * 1024)
    cells = (CX + 2) * (CY + 2)
    sums = pl.pallas_call(
        deposit_kernel,
        out_shape=jax.ShapeDtypeStruct((cells, ROWS, NZ), jnp.float32),
        grid_spec=pltpu.PrefetchScalarGridSpec(
            num_scalar_prefetch=2,
            grid=(PB // GROUP,),
            in_specs=[
                spread(rows_in),
                spread(3),
                per_block,
                per_block,
                spread(3),
                whole((hidden, rows_in)),
                whole((hidden, 1)),
                whole((hidden, hidden)),
                whole((hidden, 1)),
                whole((ROWS, hidden)),
                whole((ROWS, 1)),
            ],
            out_specs=whole((cells, ROWS, NZ)),
        ),
        compiler_params=params,
    )(
        block_ext,
        live,
        net_inputs,
        velocity,
        mass,
        height,
        cotangent,
        input_weight,
        b1,
        middle_weight,
        b2,
        w3,
        b3,
    )
    remote_params = pltpu.CompilerParams(
        collective_id=0, has_side_effects=True, vmem_limit_bytes=40 * 1024 * 1024
    )
    in_vmem = pl.BlockSpec(memory_space=pltpu.VMEM)
    wide_shape = (CX + 4, CY + 4, ROWS, NZ)
    wide, energy_tile = pl.pallas_call(
        halo_kernel,
        out_shape=(
            jax.ShapeDtypeStruct(wide_shape, jnp.float32),
            jax.ShapeDtypeStruct((8, NZ), jnp.float32),
        ),
        in_specs=[in_vmem],
        out_specs=(in_vmem, in_vmem),
        scratch_shapes=[
            pltpu.VMEM((2, 3, CY + 2, ROWS, NZ), jnp.float32),
            pltpu.VMEM((2, CX + 4, 3, ROWS, NZ), jnp.float32),
            pltpu.SemaphoreType.DMA((4,)),
            pltpu.SemaphoreType.DMA((4,)),
        ]
        + sum_scratch((8, NZ)),
        compiler_params=remote_params,
    )(sums.reshape(CX + 2, CY + 2, ROWS, NZ))
    energy = jnp.sum(energy_tile) / (width_x * width_y * NZ)
    step_size = time_scale / jnp.sqrt(energy + epsilon)

    f32 = jnp.float32
    new_velocity, gin, gmid, gout, bin_, bmid, bout = pl.pallas_call(
        gather_kernel,
        out_shape=(
            jax.ShapeDtypeStruct(velocity.shape, f32),
            jax.ShapeDtypeStruct((hidden, rows_in), f32),
            jax.ShapeDtypeStruct((hidden, hidden), f32),
            jax.ShapeDtypeStruct((hidden, ROWS), f32),
            jax.ShapeDtypeStruct((hidden, BLOCK), f32),
            jax.ShapeDtypeStruct((hidden, BLOCK), f32),
            jax.ShapeDtypeStruct((ROWS, BLOCK), f32),
        ),
        grid_spec=pltpu.PrefetchScalarGridSpec(
            num_scalar_prefetch=3,
            grid=(PB // GROUP,),
            in_specs=[
                spread(rows_in),
                per_block,
                per_block,
                whole(wide_shape),
                whole((hidden, rows_in)),
                whole((hidden, 1)),
                whole((hidden, hidden)),
                whole((hidden, 1)),
                whole((hidden, ROWS)),
                whole((hidden, hidden)),
            ],
            out_specs=(
                spread(3),
                whole((hidden, rows_in)),
                whole((hidden, hidden)),
                whole((hidden, ROWS)),
                whole((hidden, BLOCK)),
                whole((hidden, BLOCK)),
                whole((ROWS, BLOCK)),
            ),
            scratch_shapes=[
                pltpu.VMEM(wide_shape, f32),
                pltpu.VMEM((cells, ROWS, NZ), f32),
            ],
        ),
        compiler_params=params,
    )(
        block_ext,
        live,
        step_size.reshape(1),
        net_inputs,
        mass,
        height,
        wide,
        input_weight,
        b1,
        middle_weight,
        b2,
        w3.T,
        middle_weight.T,
    )
    live_total = jnp.sum(block_counts).astype(jnp.float32) * BLOCK
    scale = 1.0 / jnp.sqrt(live_total)
    joined_shape = (hidden, BLOCK)
    assert rows_in + hidden + ROWS + 3 <= BLOCK
    summed = pl.pallas_call(
        grads_kernel,
        out_shape=jax.ShapeDtypeStruct(joined_shape, f32),
        in_specs=[in_vmem] * 6,
        out_specs=in_vmem,
        scratch_shapes=sum_scratch(joined_shape),
        compiler_params=pltpu.CompilerParams(collective_id=1, has_side_effects=True),
    )(gin, gmid, gout, bin_, bmid, bout)
    summed = summed * scale
    mid = rows_in + 1
    out = mid + hidden + 1
    return (
        new_velocity,
        summed[:, 0:rows_in],
        summed[:, rows_in],
        summed[:, mid : mid + hidden],
        summed[:, mid + hidden],
        summed[:, out + 4 : out + 13].reshape(hidden, 3, 3).transpose(2, 1, 0).reshape(9, hidden),
        summed[4:13, out + ROWS].reshape(3, 3).T.reshape(9),
    )


def solution(mesh):
    return jax.shard_map(
        shards,
        mesh=mesh,
        in_specs=(
            P(None, ("gx", "gy")),
            P(None, ("gx", "gy")),
            P(("gx", "gy")),
            P(("gx", "gy")),
            P(("gx", "gy")),
            P(),
            P(None, ("gx", "gy")),
            P(),
            P(),
            P(),
            P(),
            P(),
            P(),
        ),
        out_specs=(P(None, ("gx", "gy")), P(), P(), P(), P(), P(), P()),
        check_vma=False,
    )
```

```python
import jax
import jax.numpy as jnp
from jax import lax
from jax.experimental import pallas as pl
from jax.experimental.pallas import tpu as pltpu
from jax.sharding import PartitionSpec as P

CX = 16
CY = 16
NZ = 128
PB = 384
BLOCK = 128
GROUP = 16
ROWS = 16
SPAN = GROUP * BLOCK


time_scale = 0.5
epsilon = 1e-06


def sigmoid(values):
    return 0.5 * jnp.tanh(0.5 * values) + 0.5


def dot(left, right):
    return jnp.dot(left, right, preferred_element_type=jnp.float32)


def dot_nt(left, right):
    return lax.dot_general(
        left, right, (((1,), (1,)), ((), ())), preferred_element_type=jnp.float32
    )


def split_halves(values):
    high = values.astype(jnp.bfloat16)
    low = (values - high.astype(jnp.float32)).astype(jnp.bfloat16)
    return jnp.concatenate([high, low], axis=0)


def height_selector(heights):
    level = lax.broadcasted_iota(jnp.int32, (NZ, BLOCK), 0)
    return jnp.where(level == heights, 1.0, 0.0).astype(jnp.bfloat16)


def deposit_kernel(
    column_ref,
    live_ref,
    inputs_ref,
    velocity_ref,
    mass_ref,
    height_ref,
    cot_ref,
    w1_ref,
    b1_ref,
    w2_ref,
    b2_ref,
    w3_ref,
    b3_ref,
    sums_ref,
):
    turn = pl.program_id(0)

    @pl.when(turn == 0)
    def _():
        sums_ref[...] = jnp.zeros_like(sums_ref)

    first = dot(w1_ref[...], inputs_ref[...]) + b1_ref[...]
    first_act = (first * sigmoid(first)).astype(jnp.bfloat16)
    second = dot(w2_ref[...], first_act) + b2_ref[...]
    second_act = (second * sigmoid(second)).astype(jnp.bfloat16)
    stress = dot(w3_ref[...], second_act) + b3_ref[...]
    gap = jnp.zeros((ROWS - 6, SPAN), jnp.float32)
    values = stress + jnp.concatenate([velocity_ref[...], gap, cot_ref[...]], axis=0)
    weighted = lax.broadcasted_iota(jnp.int32, (ROWS, BLOCK), 0) < 13
    for block in range(GROUP):
        index = turn * GROUP + block
        live = jnp.where(index < live_ref[0], 1.0, 0.0)
        weight = mass_ref[block : block + 1, :] * live
        piece = values[:, block * BLOCK : (block + 1) * BLOCK] * jnp.where(weighted, weight, 1.0)
        selector = height_selector(height_ref[block : block + 1, :])
        both = dot_nt(split_halves(piece), selector)
        column = column_ref[index]
        sums_ref[column] = sums_ref[column] + (both[:ROWS] + both[ROWS:])


def fill_grid(step, wide_ref, scaled_ref, grid_ref):
    wide_x, wide_y = CX + 4, CY + 4
    cots = lax.broadcasted_iota(jnp.int32, (wide_y, ROWS, NZ), 1) >= 13
    lane = lax.broadcasted_iota(jnp.int32, (CY + 2, ROWS, NZ), 2)

    def scale_row(x, carry):
        totals = wide_ref[x]
        inverse = 1.0 / (totals[:, 3:4] + 1.0)
        scaled_ref[x] = totals * jnp.where(cots, inverse, 1.0)
        return carry

    lax.fori_loop(0, wide_x, scale_row, 0)

    def fill_row(x, carry):
        here = scaled_ref[x + 1]
        middle = here[1:-1]
        diff_x = 0.5 * (scaled_ref[x + 2, 1 : wide_y - 1] - scaled_ref[x, 1 : wide_y - 1])
        diff_y = 0.5 * (here[2:] - here[:-2])
        above = jnp.where(lane < NZ - 1, pltpu.roll(middle, NZ - 1, 2), 0.0)
        below = jnp.where(lane > 0, pltpu.roll(middle, 1, 2), 0.0)
        diff_z = 0.5 * (above - below)
        inverse = 1.0 / (middle[:, 3:4] + 1.0)
        force = diff_x[:, 4:7] + diff_y[:, 7:10] + diff_z[:, 10:13]
        speed = inverse * middle[:, 0:3] + step * (inverse * force)
        cot_rows = [-step * diff[:, 13:16] for diff in (diff_x, diff_y, diff_z)]
        rows = jnp.concatenate(
            [speed, jnp.zeros_like(inverse)] + cot_rows + [jnp.zeros_like(speed)], axis=1
        )
        grid_ref[pl.ds(x * (CY + 2), CY + 2)] = rows
        return carry

    lax.fori_loop(0, CX + 2, fill_row, 0)


def gather_kernel(
    column_ref,
    live_ref,
    step_ref,
    inputs_ref,
    mass_ref,
    height_ref,
    wide_ref,
    w1_ref,
    b1_ref,
    w2_ref,
    b2_ref,
    w3t_ref,
    w2t_ref,
    velocity_ref,
    gin_ref,
    gmid_ref,
    gout_ref,
    bin_ref,
    bmid_ref,
    bout_ref,
    scaled_ref,
    grid_ref,
):
    turn = pl.program_id(0)
    step = step_ref[0]

    @pl.when(turn == 0)
    def _():
        for ref in (gin_ref, gmid_ref, gout_ref, bin_ref, bmid_ref, bout_ref):
            ref[...] = jnp.zeros_like(ref)
        fill_grid(step, wide_ref, scaled_ref, grid_ref)

    picked_cols, cot_cols = [], []
    for block in range(GROUP):
        index = turn * GROUP + block
        live = jnp.where(index < live_ref[0], 1.0, 0.0)
        weight = mass_ref[block : block + 1, :] * live
        selector = height_selector(height_ref[block : block + 1, :])
        both = dot(split_halves(grid_ref[column_ref[index]]), selector)
        picked = both[:ROWS] + both[ROWS:]
        picked_cols.append(picked)
        cot_cols.append(picked * weight)
    picked = jnp.concatenate(picked_cols, axis=1)
    stress_cot = jnp.concatenate(cot_cols, axis=1)
    velocity_ref[...] = picked[0:3]

    inputs = inputs_ref[...]
    first = dot(w1_ref[...], inputs) + b1_ref[...]
    first_sig = sigmoid(first)
    first_act = (first * first_sig).astype(jnp.bfloat16)
    second = dot(w2_ref[...], first_act) + b2_ref[...]
    second_sig = sigmoid(second)
    second_act = (second * second_sig).astype(jnp.bfloat16)
    cot_low = stress_cot.astype(jnp.bfloat16)
    second_cot = dot(w3t_ref[...], cot_low) * (second_sig * (1.0 + second * (1.0 - second_sig)))
    second_low = second_cot.astype(jnp.bfloat16)
    first_cot = dot(w2t_ref[...], second_low) * (first_sig * (1.0 + first * (1.0 - first_sig)))
    first_low = first_cot.astype(jnp.bfloat16)
    gin_ref[...] += dot_nt(first_low, inputs)
    gmid_ref[...] += dot_nt(second_low, first_act)
    gout_ref[...] += dot_nt(second_act, cot_low)

    def lanes(values):
        return sum(values[:, k * BLOCK : (k + 1) * BLOCK] for k in range(GROUP))

    bin_ref[...] += lanes(first_cot)
    bmid_ref[...] += lanes(second_cot)
    bout_ref[...] += lanes(stress_cot)


def greet_lines(me_x, me_y, size_x, size_y):
    barrier = pltpu.get_barrier_semaphore()
    for d in range(1, size_y):
        pl.semaphore_signal(
            barrier,
            inc=1,
            device_id=(me_x, lax.rem(me_y + d, size_y)),
            device_id_type=pl.DeviceIdType.MESH,
        )
    for d in range(1, size_x):
        pl.semaphore_signal(
            barrier,
            inc=1,
            device_id=(lax.rem(me_x + d, size_x), me_y),
            device_id_type=pl.DeviceIdType.MESH,
        )
    pl.semaphore_wait(barrier, size_x + size_y - 2)


def remote(source, target, send, recv, device):
    return pltpu.make_async_remote_copy(
        src_ref=source,
        dst_ref=target,
        send_sem=send,
        recv_sem=recv,
        device_id=device,
        device_id_type=pl.DeviceIdType.MESH,
    )


def line_sum(slots, send, recv, me, size, target):
    copies = []
    for d in range(1, size):
        copy = remote(
            slots.at[me], slots.at[me], send.at[d], recv.at[me], target(lax.rem(me + d, size))
        )
        copy.start()
        copies.append(copy)
    for d in range(1, size):
        other = lax.rem(me + d, size)
        remote(
            slots.at[other], slots.at[other], send.at[d], recv.at[other], target(other)
        ).wait_recv()
    for copy in copies:
        copy.wait_send()
    total = slots[0]
    for k in range(1, size):
        total = total + slots[k]
    return total


def mesh_sum(values, y_slots, x_slots, y_send, y_recv, x_send, x_recv):
    me_x, me_y = lax.axis_index("gx"), lax.axis_index("gy")
    y_slots[me_y] = values
    x_slots[me_x] = line_sum(
        y_slots, y_send, y_recv, me_y, y_slots.shape[0], lambda other: (me_x, other)
    )
    return line_sum(x_slots, x_send, x_recv, me_x, x_slots.shape[0], lambda other: (other, me_y))


def sum_scratch(shape):
    size_x, size_y = lax.axis_size("gx"), lax.axis_size("gy")
    return [
        pltpu.VMEM((size_y,) + shape, jnp.float32),
        pltpu.VMEM((size_x,) + shape, jnp.float32),
        pltpu.SemaphoreType.DMA((size_y,)),
        pltpu.SemaphoreType.DMA((size_y,)),
        pltpu.SemaphoreType.DMA((size_x,)),
        pltpu.SemaphoreType.DMA((size_x,)),
    ]


def grads_kernel(gin_ref, gmid_ref, gout_ref, bin_ref, bmid_ref, bout_ref, out_ref, *slots):
    size_x, size_y = slots[1].shape[0], slots[0].shape[0]
    greet_lines(lax.axis_index("gx"), lax.axis_index("gy"), size_x, size_y)
    hidden = gin_ref.shape[0]
    bout = jnp.sum(bout_ref[...], axis=1, keepdims=True)
    parts = [
        gin_ref[...],
        jnp.sum(bin_ref[...], axis=1, keepdims=True),
        gmid_ref[...],
        jnp.sum(bmid_ref[...], axis=1, keepdims=True),
        gout_ref[...],
        jnp.concatenate([bout, jnp.zeros((hidden - ROWS, 1), jnp.float32)], axis=0),
    ]
    gap = out_ref.shape[1] - sum(part.shape[1] for part in parts)
    joined = jnp.concatenate(parts + [jnp.zeros((hidden, gap), jnp.float32)], axis=1)
    out_ref[...] = mesh_sum(joined, *slots)


def halo_kernel(
    sums_ref, wide_ref, energy_ref, x_halo, y_halo, halo_send, halo_recv, *slots
):
    size_x, size_y = slots[1].shape[0], slots[0].shape[0]
    me_x, me_y = lax.axis_index("gx"), lax.axis_index("gy")
    greet_lines(me_x, me_y, size_x, size_y)
    next_x, last_x = lax.rem(me_x + 1, size_x), lax.rem(me_x + size_x - 1, size_x)
    next_y, last_y = lax.rem(me_y + 1, size_y), lax.rem(me_y + size_y - 1, size_y)
    ends = CX + 2
    copies = [
        remote(
            sums_ref.at[pl.ds(ends - 3, 3)],
            x_halo.at[0],
            halo_send.at[0],
            halo_recv.at[0],
            (next_x, me_y),
        ),
        remote(
            sums_ref.at[pl.ds(0, 3)], x_halo.at[1], halo_send.at[1], halo_recv.at[1], (last_x, me_y)
        ),
    ]
    edge = CY + 2
    still, still_wide = pl.ds(2, CX - 2), pl.ds(3, CX - 2)
    early = [
        remote(
            sums_ref.at[still, pl.ds(edge - 3, 3)],
            y_halo.at[0, still_wide],
            halo_send.at[2],
            halo_recv.at[2],
            (me_x, next_y),
        ),
        remote(
            sums_ref.at[still, pl.ds(0, 3)],
            y_halo.at[1, still_wide],
            halo_send.at[3],
            halo_recv.at[3],
            (me_x, last_y),
        ),
    ]
    for copy in copies + early:
        copy.start()
    inner_y = pl.ds(1, CY + 2)

    def move(x, carry):
        wide_ref[x + 1, inner_y] = sums_ref[x]
        return carry

    lax.fori_loop(2, ends - 2, move, 0)
    for copy in copies:
        copy.wait()
    wide_ref[0, inner_y] = x_halo[0, 0]
    wide_ref[1, inner_y] = sums_ref[0] + x_halo[0, 1]
    wide_ref[2, inner_y] = sums_ref[1] + x_halo[0, 2]
    wide_ref[ends - 1, inner_y] = sums_ref[ends - 2] + x_halo[1, 0]
    wide_ref[ends, inner_y] = sums_ref[ends - 1] + x_halo[1, 1]
    wide_ref[ends + 1, inner_y] = x_halo[1, 2]
    copies = []
    for k, rows in enumerate((pl.ds(0, 3), pl.ds(CX + 1, 3))):
        for side, start, device in ((0, edge - 2, next_y), (1, 1, last_y)):
            number = 4 + 2 * k + side
            copies.append(
                remote(
                    wide_ref.at[rows, pl.ds(start, 3)],
                    y_halo.at[side, rows],
                    halo_send.at[number],
                    halo_recv.at[number],
                    (me_x, device),
                )
            )
    for copy in copies:
        copy.start()
    for copy in early + copies:
        copy.wait()

    def fold(x, carry):
        wide_ref[x, 0] = y_halo[0, x, 0]
        wide_ref[x, 1] = wide_ref[x, 1] + y_halo[0, x, 1]
        wide_ref[x, 2] = wide_ref[x, 2] + y_halo[0, x, 2]
        wide_ref[x, edge - 1] = wide_ref[x, edge - 1] + y_halo[1, x, 0]
        wide_ref[x, edge] = wide_ref[x, edge] + y_halo[1, x, 1]
        wide_ref[x, edge + 1] = y_halo[1, x, 2]
        return carry

    lax.fori_loop(0, CX + 4, fold, 0)
    speeds = lax.broadcasted_iota(jnp.int32, (8, NZ), 0) < 3

    def energy_row(x, total):
        cells = wide_ref[x, 2 : CY + 2, 0:8]
        drift = cells * (1.0 / (cells[:, 3:4] + 1.0))
        return total + jnp.sum(drift * drift, axis=0)

    energy = lax.fori_loop(2, CX + 2, energy_row, jnp.zeros((8, NZ), jnp.float32))
    energy_ref[...] = mesh_sum(jnp.where(speeds, energy, 0.0), *slots)


def shards(
    net_inputs,
    velocity,
    particle_mass,
    block_column,
    cell_height,
    block_counts,
    cotangent,
    input_weight,
    input_bias,
    middle_weight,
    middle_bias,
    output_weight,
    output_bias,
):
    tiles_x, tiles_y = lax.axis_size("gx"), lax.axis_size("gy")
    index_x, index_y = lax.axis_index("gx"), lax.axis_index("gy")
    width_x, width_y = CX * tiles_x, CY * tiles_y
    hidden, rows_in = input_weight.shape
    live = lax.dynamic_slice_in_dim(block_counts, index_x * tiles_y + index_y, 1, 0)
    local_x = (block_column // width_y - index_x * CX + 1) % width_x
    local_y = (block_column % width_y - index_y * CY + 1) % width_y
    block_ext = local_x * (CY + 2) + local_y
    mass = particle_mass.reshape(PB, BLOCK)
    height = cell_height.reshape(PB, BLOCK)
    b1 = input_bias[:, None]
    b2 = middle_bias[:, None]
    turned = output_weight.reshape(3, 3, hidden).transpose(1, 0, 2).reshape(9, hidden)
    w3 = jnp.pad(turned, ((4, 3), (0, 0)))
    b3 = jnp.concatenate(
        [jnp.zeros((3,)), jnp.ones((1,)), output_bias.reshape(3, 3).T.reshape(9), jnp.zeros((3,))]
    ).astype(jnp.float32)[:, None]

    def whole(shape):
        return pl.BlockSpec(shape, lambda i, *_: (0,) * len(shape))

    def spread(rows):
        return pl.BlockSpec((rows, SPAN), lambda i, *_: (0, i))

    per_block = pl.BlockSpec((GROUP, BLOCK), lambda i, *_: (i, 0))
    params = pltpu.CompilerParams(vmem_limit_bytes=40 * 1024 * 1024)
    cells = (CX + 2) * (CY + 2)
    sums = pl.pallas_call(
        deposit_kernel,
        out_shape=jax.ShapeDtypeStruct((cells, ROWS, NZ), jnp.float32),
        grid_spec=pltpu.PrefetchScalarGridSpec(
            num_scalar_prefetch=2,
            grid=(PB // GROUP,),
            in_specs=[
                spread(rows_in),
                spread(3),
                per_block,
                per_block,
                spread(3),
                whole((hidden, rows_in)),
                whole((hidden, 1)),
                whole((hidden, hidden)),
                whole((hidden, 1)),
                whole((ROWS, hidden)),
                whole((ROWS, 1)),
            ],
            out_specs=whole((cells, ROWS, NZ)),
        ),
        compiler_params=params,
    )(
        block_ext,
        live,
        net_inputs,
        velocity,
        mass,
        height,
        cotangent,
        input_weight,
        b1,
        middle_weight,
        b2,
        w3,
        b3,
    )
    remote_params = pltpu.CompilerParams(
        collective_id=0, has_side_effects=True, vmem_limit_bytes=40 * 1024 * 1024
    )
    in_vmem = pl.BlockSpec(memory_space=pltpu.VMEM)
    wide_shape = (CX + 4, CY + 4, ROWS, NZ)
    wide, energy_tile = pl.pallas_call(
        halo_kernel,
        out_shape=(
            jax.ShapeDtypeStruct(wide_shape, jnp.float32),
            jax.ShapeDtypeStruct((8, NZ), jnp.float32),
        ),
        in_specs=[in_vmem],
        out_specs=(in_vmem, in_vmem),
        scratch_shapes=[
            pltpu.VMEM((2, 3, CY + 2, ROWS, NZ), jnp.float32),
            pltpu.VMEM((2, CX + 4, 3, ROWS, NZ), jnp.float32),
            pltpu.SemaphoreType.DMA((8,)),
            pltpu.SemaphoreType.DMA((8,)),
        ]
        + sum_scratch((8, NZ)),
        compiler_params=remote_params,
    )(sums.reshape(CX + 2, CY + 2, ROWS, NZ))
    energy = jnp.sum(energy_tile) / (width_x * width_y * NZ)
    step_size = time_scale / jnp.sqrt(energy + epsilon)

    f32 = jnp.float32
    new_velocity, gin, gmid, gout, bin_, bmid, bout = pl.pallas_call(
        gather_kernel,
        out_shape=(
            jax.ShapeDtypeStruct(velocity.shape, f32),
            jax.ShapeDtypeStruct((hidden, rows_in), f32),
            jax.ShapeDtypeStruct((hidden, hidden), f32),
            jax.ShapeDtypeStruct((hidden, ROWS), f32),
            jax.ShapeDtypeStruct((hidden, BLOCK), f32),
            jax.ShapeDtypeStruct((hidden, BLOCK), f32),
            jax.ShapeDtypeStruct((ROWS, BLOCK), f32),
        ),
        grid_spec=pltpu.PrefetchScalarGridSpec(
            num_scalar_prefetch=3,
            grid=(PB // GROUP,),
            in_specs=[
                spread(rows_in),
                per_block,
                per_block,
                whole(wide_shape),
                whole((hidden, rows_in)),
                whole((hidden, 1)),
                whole((hidden, hidden)),
                whole((hidden, 1)),
                whole((hidden, ROWS)),
                whole((hidden, hidden)),
            ],
            out_specs=(
                spread(3),
                whole((hidden, rows_in)),
                whole((hidden, hidden)),
                whole((hidden, ROWS)),
                whole((hidden, BLOCK)),
                whole((hidden, BLOCK)),
                whole((ROWS, BLOCK)),
            ),
            scratch_shapes=[
                pltpu.VMEM(wide_shape, f32),
                pltpu.VMEM((cells, ROWS, NZ), f32),
            ],
        ),
        compiler_params=params,
    )(
        block_ext,
        live,
        step_size.reshape(1),
        net_inputs,
        mass,
        height,
        wide,
        input_weight,
        b1,
        middle_weight,
        b2,
        w3.T,
        middle_weight.T,
    )
    live_total = jnp.sum(block_counts).astype(jnp.float32) * BLOCK
    scale = 1.0 / jnp.sqrt(live_total)
    joined_shape = (hidden, BLOCK)
    assert rows_in + hidden + ROWS + 3 <= BLOCK
    summed = pl.pallas_call(
        grads_kernel,
        out_shape=jax.ShapeDtypeStruct(joined_shape, f32),
        in_specs=[in_vmem] * 6,
        out_specs=in_vmem,
        scratch_shapes=sum_scratch(joined_shape),
        compiler_params=pltpu.CompilerParams(collective_id=1, has_side_effects=True),
    )(gin, gmid, gout, bin_, bmid, bout)
    summed = summed * scale
    mid = rows_in + 1
    out = mid + hidden + 1
    return (
        new_velocity,
        summed[:, 0:rows_in],
        summed[:, rows_in],
        summed[:, mid : mid + hidden],
        summed[:, mid + hidden],
        summed[:, out + 4 : out + 13].reshape(hidden, 3, 3).transpose(2, 1, 0).reshape(9, hidden),
        summed[4:13, out + ROWS].reshape(3, 3).T.reshape(9),
    )


def solution(mesh):
    return jax.shard_map(
        shards,
        mesh=mesh,
        in_specs=(
            P(None, ("gx", "gy")),
            P(None, ("gx", "gy")),
            P(("gx", "gy")),
            P(("gx", "gy")),
            P(("gx", "gy")),
            P(),
            P(None, ("gx", "gy")),
            P(),
            P(),
            P(),
            P(),
            P(),
            P(),
        ),
        out_specs=(P(None, ("gx", "gy")), P(), P(), P(), P(), P(), P()),
        check_vma=False,
    )
```
